32 devices in a mesh: groups: 2 (over y), leaf: 4 (over z), sample: 4 (over x, core).
Axes of the slice: x: 2, y: 2, z: 4, core: 2. Of those that a mesh axis runs over, the one named last changes fastest.
Arguments:
- points: bfloat16 [16384, 256], P(('groups', 'leaf', 'sample')), parts along dimension 0, may hold values from -40 to 40
- cotangent: bfloat16 [16384, 256], P(('groups', 'leaf', 'sample')), parts along dimension 0, may hold values from -6 to 6
- dest_pos: int32 [16384], P(('groups', 'leaf', 'sample')), parts along dimension 0, may hold values from 0 to 8191, as said below
- w_qkv: bfloat16 [256, 768], replicated, may hold values from -8 to 8
- w_out: bfloat16 [256, 256], replicated, may hold values from -0.375 to 0.375
- w_up: bfloat16 [256, 1024], replicated, may hold values from -0.375 to 0.375
- w_down: bfloat16 [1024, 256], replicated, may hold values from -0.1875 to 0.1875
- gain_attn: float32 [256], replicated, may hold values from 0.1 to 1.9
- gain_mlp: float32 [256], replicated, may hold values from 0.1 to 1.9
Outputs:
- grad_points: bfloat16 [16384, 256], P(('groups', 'leaf', 'sample')), parts along dimension 0
- grad_w_qkv: float32 [512, 768], P(('groups', 'leaf')), parts along dimension 0
- grad_w_out: float32 [512, 256], P(('groups', 'leaf')), parts along dimension 0
- grad_w_up: float32 [512, 1024], P(('groups', 'leaf')), parts along dimension 0
- grad_w_down: float32 [2048, 256], P(('groups', 'leaf')), parts along dimension 0
- grad_gain_attn: float32 [512], P(('groups', 'leaf')), parts along dimension 0
- grad_gain_mlp: float32 [512], P(('groups', 'leaf')), parts along dimension 0
The draws below stay inside these ranges and needn't reach their ends.
There are 2 independent parts, one for each index of `groups`. The reference program is written for one: setup_inputs(seed, part) draws one part's arguments, and reference() takes and returns one part's arrays. A program takes and returns all parts, laid end to end along the dimension named above; an argument that names none is the same for every part. Nothing has to cross between parts.
Inputs may be any that keep to these rules, and one draw needn't show every extreme that they name: `dest_pos`: a permutation of the 8192 positions; of the 512 points of one device, at most 64 have positions in any one aligned block of 512 positions, and in every draw some device reaches exactly 64 for some block.
All inputs are finite; a program needn't handle non-finite values.
Results may differ from the reference program's by a relative error of at most 0.0059.
The reference program's roundings to bfloat16 on the way count: a program that leaves them out, or rounds other values in their place, can miss the bound.
Values may be sent and summed in bfloat16 or wider, within the bound.
A program may use at most 64 MiB of HBM per device.

```python
import math
import jax
import jax.numpy as jnp
from jax import lax

D = 256
HEADS = 8
FF = 1024
BALL = 256
PTS_DEV = 512
HEAD_DIM = 32
PEERS = 16
POINTS = 8192


def draw_points(key, part):
    key_base, key_rows, key_cols = jax.random.split(key, 3)
    row_scale = jnp.exp(jax.random.uniform(key_rows, (POINTS, 1), minval=0.0, maxval=math.log(10.0)))
    col_scale = jnp.exp(jax.random.uniform(key_cols, (1, D), minval=math.log(0.5), maxval=math.log(2.0)))
    base = jax.random.normal(key_base, (POINTS, D))
    return jnp.clip(base * row_scale * col_scale, -40.0, 40.0).astype(jnp.bfloat16)


def draw_w_qkv(key, part):
    key_base = jax.random.fold_in(key, 0)
    base = jax.random.normal(key_base, (D, 3 * D)) * D ** (-0.5)
    return jnp.clip(base, -8.0, 8.0).astype(jnp.bfloat16)


def pair_profile(first_key, second_key):
    half_pair = PTS_DEV // PEERS // 2
    offsets = jax.random.randint(first_key, (PEERS // 2,), 0, half_pair + 1).astype(jnp.int32)
    offsets = offsets.at[0].set(half_pair)
    paired = jnp.stack([half_pair + offsets, half_pair - offsets], axis=1).reshape(PEERS)
    return paired[jax.random.permutation(second_key, PEERS)]


def draw_dest_pos(key, part):
    keys_all = jax.random.split(key, 6)
    first_prof = pair_profile(keys_all[0], keys_all[1])
    second_prof = pair_profile(keys_all[2], keys_all[3])
    first_top = jnp.argmax(first_prof).astype(jnp.int32)
    second_top = jnp.argmax(second_prof).astype(jnp.int32)
    second_prof = jnp.where((first_top - second_top) % 2 == 0, second_prof, jnp.roll(second_prof, 1))
    source_dev = jnp.arange(PEERS, dtype=jnp.int32)[:, None]
    dest_dev = jnp.arange(PEERS, dtype=jnp.int32)[None, :]
    counts = first_prof[(dest_dev - source_dev) % PEERS] + second_prof[(dest_dev + source_dev) % PEERS]
    row_end = jnp.cumsum(counts, axis=1)
    row_start = row_end - counts
    col_start = jnp.cumsum(counts, axis=0) - counts
    local_rank = jnp.arange(PTS_DEV, dtype=jnp.int32)
    dest_of = jax.vmap(lambda row_ends: jnp.searchsorted(row_ends, local_rank, side='right'))(row_end).astype(jnp.int32)
    within = local_rank[None, :] - jnp.take_along_axis(row_start, dest_of, axis=1) + jnp.take_along_axis(col_start, dest_of, axis=1)
    shuffles = jax.vmap(lambda sub_key: jax.random.permutation(sub_key, PTS_DEV))(jax.random.split(keys_all[4], PEERS)).astype(jnp.int32)
    slot_local = shuffles[dest_of, within]
    positions = dest_of * PTS_DEV + slot_local
    src_perms = jax.vmap(lambda sub_key: jax.random.permutation(sub_key, PTS_DEV))(jax.random.split(keys_all[5], PEERS)).astype(jnp.int32)
    result = jnp.zeros((PEERS, PTS_DEV), jnp.int32).at[jnp.arange(PEERS, dtype=jnp.int32)[:, None], src_perms].set(positions)
    return result.reshape(POINTS).astype(jnp.int32)


def block_levels(stream_key, extent, cuts, smallest, largest):
    def one(dim, parts):
        steps = jax.random.uniform(jax.random.fold_in(jax.random.fold_in(stream_key, 6), dim), (parts,), jnp.float32, smallest / len(cuts), largest / len(cuts))
        return jnp.repeat(jnp.exp(steps), extent[dim] // parts).reshape((-1,) + (1,) * (len(extent) - dim - 1))

    level = one(*cuts[0])
    for cut in cuts[1:]:
        level = level * one(*cut)
    return level


def scatter_about(rng, shape, spread, reach, cuts=(), held_as=jnp.bfloat16):
    values = jax.random.normal(rng, shape, jnp.float32) * spread
    if len(cuts) > 0:
        values = block_levels(rng, shape, cuts, -0.22, 0.18) * values
    return jnp.clip(values, min=-reach, max=reach).astype(held_as)


def setup_inputs(seed: int = 0, part: int = 0) -> dict:
    seeds = jax.random.split(jax.random.key(seed), 10)
    own_keys = jax.random.split(jax.random.fold_in(seeds[9], part), 10)
    points = draw_points(jax.random.fold_in(jax.random.fold_in(seeds[9], part), 71), part)
    cotangent = scatter_about(own_keys[1], (POINTS, D), 1.0, 6.0, ((0, 16),))
    dest_pos = draw_dest_pos(jax.random.fold_in(jax.random.fold_in(seeds[9], part), 71), part)
    w_qkv = draw_w_qkv(jax.random.fold_in(seeds[9], 71), part)
    w_out = scatter_about(seeds[4], (D, D), D ** -0.5, 0.375)
    w_up = scatter_about(seeds[5], (D, FF), D ** -0.5, 0.375)
    w_down = scatter_about(seeds[6], (FF, D), FF ** -0.5, 0.1875)
    gain_attn = jnp.clip(1.0 + 0.18 * jax.random.normal(seeds[7], (D,), jnp.float32), 0.1, 1.9)
    gain_mlp = jnp.clip(1.0 + 0.18 * jax.random.normal(seeds[8], (D,), jnp.float32), 0.1, 1.9)
    return dict(points=points, cotangent=cotangent, dest_pos=dest_pos, w_qkv=w_qkv, w_out=w_out, w_up=w_up, w_down=w_down, gain_attn=gain_attn, gain_mlp=gain_mlp)


EPSILON = 1e-06
GELU_COEF = math.sqrt(2.0 / math.pi)

def to_low(matrix):
    return lax.optimization_barrier(matrix.astype(jnp.bfloat16))

def rms_scale(matrix):
    return lax.rsqrt(lax.optimization_barrier(jnp.mean(matrix * matrix, axis=1, keepdims=True)) + EPSILON)

def gelu_parts(pre_act):
    tanh_val = jnp.tanh(GELU_COEF * (pre_act + 0.044715 * pre_act * pre_act * pre_act))
    value = 0.5 * pre_act * (1.0 + tanh_val)
    slope = 0.5 * (1.0 + tanh_val) + 0.5 * pre_act * (1.0 - tanh_val * tanh_val) * GELU_COEF * (1.0 + 3.0 * 0.044715 * pre_act * pre_act)
    return (value, slope)

def ball_split(ball_block):
    ball_groups = ball_block.shape[0] // BALL
    split_parts = ball_block.astype(jnp.float32).reshape(ball_groups, BALL, 3, HEADS, HEAD_DIM)
    return (split_parts[:, :, 0], split_parts[:, :, 1], split_parts[:, :, 2])

def softmax_probs(queries, key_rows):
    scores = jnp.einsum('gqhd,gkhd->ghqk', queries, key_rows) * HEAD_DIM ** (-0.5)
    return jax.nn.softmax(scores, axis=-1)

def ball_forward(operands):
    queries, key_rows, values = ball_split(operands[0])
    probs_low = to_low(softmax_probs(queries, key_rows)).astype(jnp.float32)
    mixed = jnp.einsum('ghqk,gkhd->gqhd', probs_low, values)
    return mixed.reshape(-1, HEADS * HEAD_DIM).astype(jnp.bfloat16)

def ball_backward(operands):
    ball_block, grad_block = operands
    queries, key_rows, values = ball_split(ball_block)
    attn_probs = softmax_probs(queries, key_rows)
    probs_low = to_low(attn_probs).astype(jnp.float32)
    upstream = grad_block.astype(jnp.float32).reshape(queries.shape)
    grad_values = jnp.einsum('ghqk,gqhd->gkhd', probs_low, upstream)
    grad_probs = jnp.einsum('gqhd,gkhd->ghqk', upstream, values)
    row_delta = lax.optimization_barrier(jnp.sum(grad_probs * attn_probs, axis=-1, keepdims=True))
    grad_scores = to_low(attn_probs * (grad_probs - row_delta)).astype(jnp.float32)
    grad_queries = jnp.einsum('ghqk,gkhd->gqhd', grad_scores, key_rows) * HEAD_DIM ** (-0.5)
    grad_keys = jnp.einsum('ghqk,gqhd->gkhd', grad_scores, queries) * HEAD_DIM ** (-0.5)
    stacked = jnp.stack([grad_queries, grad_keys, grad_values], axis=2)
    return stacked.reshape(-1, 3 * HEADS * HEAD_DIM).astype(jnp.bfloat16)

def over_balls(function, operands):
    row_count = operands[0].shape[0]
    ball_count = row_count // BALL
    per_group = math.gcd(ball_count, max(1, 512 // BALL))
    shaped = tuple((operand.reshape(ball_count // per_group, per_group * BALL, operand.shape[1]) for operand in operands))
    result = lax.map(function, shaped)
    return result.reshape(row_count, result.shape[2])

def layer_grads(rotated, rot_cot, w_qkv, w_out, w_up, w_down, gain_attn, gain_mlp):
    rotated_f = rotated.astype(jnp.float32)
    scale_one = rms_scale(rotated_f)
    norm_one = rotated_f * scale_one
    normed_one = to_low(norm_one * gain_attn)
    qkv_rows = to_low(jnp.dot(normed_one, w_qkv, preferred_element_type=jnp.float32))
    attended = to_low(over_balls(ball_forward, (qkv_rows,)))
    middle = rotated_f + jnp.dot(attended, w_out, preferred_element_type=jnp.float32)
    scale_two = rms_scale(middle)
    norm_two = middle * scale_two
    normed_two = to_low(norm_two * gain_mlp)
    pre_act = jnp.dot(normed_two, w_up, preferred_element_type=jnp.float32)
    act_value, act_slope = gelu_parts(pre_act)
    hidden = to_low(act_value)
    grad_down = jnp.dot(hidden.T, rot_cot, preferred_element_type=jnp.float32)
    grad_pre = to_low(jnp.dot(rot_cot, w_down.T, preferred_element_type=jnp.float32) * act_slope)
    grad_up = jnp.dot(normed_two.T, grad_pre, preferred_element_type=jnp.float32)
    grad_normed_two = jnp.dot(grad_pre, w_up.T, preferred_element_type=jnp.float32)
    grad_gain_two = lax.optimization_barrier(jnp.sum(grad_normed_two * norm_two, axis=0))
    inner_two = grad_normed_two * gain_mlp
    grad_middle = rot_cot.astype(jnp.float32) + scale_two * (inner_two - norm_two * lax.optimization_barrier(jnp.mean(inner_two * norm_two, axis=1, keepdims=True)))
    grad_middle_low = to_low(grad_middle)
    grad_out = jnp.dot(attended.T, grad_middle_low, preferred_element_type=jnp.float32)
    grad_attended = to_low(jnp.dot(grad_middle_low, w_out.T, preferred_element_type=jnp.float32))
    grad_qkv_rows = to_low(over_balls(ball_backward, (qkv_rows, grad_attended)))
    grad_qkv = jnp.dot(normed_one.T, grad_qkv_rows, preferred_element_type=jnp.float32)
    grad_normed_one = jnp.dot(grad_qkv_rows, w_qkv.T, preferred_element_type=jnp.float32)
    grad_gain_one = lax.optimization_barrier(jnp.sum(grad_normed_one * norm_one, axis=0))
    inner_one = grad_normed_one * gain_attn
    grad_rot = grad_middle + scale_one * (inner_one - norm_one * lax.optimization_barrier(jnp.mean(inner_one * norm_one, axis=1, keepdims=True)))
    return (grad_rot, grad_qkv, grad_out, grad_up, grad_down, grad_gain_one, grad_gain_two)

def reference(points, cotangent, dest_pos, w_qkv, w_out, w_up, w_down, gain_attn, gain_mlp):
    rotated = jnp.zeros_like(points).at[dest_pos].set(points)
    rot_cot = jnp.zeros_like(cotangent).at[dest_pos].set(cotangent)
    grad_rot, grad_qkv, grad_out, grad_up, grad_down, grad_gain_one, grad_gain_two = layer_grads(rotated, rot_cot, w_qkv, w_out, w_up, w_down, gain_attn, gain_mlp)
    grad_points = grad_rot[dest_pos].astype(jnp.bfloat16)
    inv_root = 1.0 / math.sqrt(POINTS)
    return (grad_points, grad_qkv * inv_root, grad_out * inv_root, grad_up * inv_root, grad_down * inv_root, grad_gain_one * inv_root, grad_gain_two * inv_root)
```

```python
import math

import jax
import jax.numpy as jnp
from jax import lax
from jax.experimental import pallas as pl
from jax.experimental.pallas import tpu as pltpu
from jax.sharding import PartitionSpec as P

HEADS = 8
BALL = 256
HEAD_DIM = 32
EPSILON = 1e-06
GELU_COEF = math.sqrt(2.0 / math.pi)
LANES = 256
MESH = pl.DeviceIdType.MESH
F32 = jnp.float32
BF16 = jnp.bfloat16


class Sizes:
    def __init__(self, mesh, rows, feat, hid):
        self.leaf = mesh.shape["leaf"]
        self.sample = mesh.shape["sample"]
        self.peers = self.leaf * self.sample
        self.rows = rows
        self.feat = feat
        self.hid = hid
        self.cap = max(16, 2 * rows // self.peers)
        self.slots = self.peers * self.cap
        self.groups = self.slots // LANES
        self.block = feat // self.leaf
        self.wire = BF16 if self.block % 16 == 0 else F32
        self.down = hid // self.peers
        self.inv_root = 1.0 / math.sqrt(rows * self.peers)


def dot(a, b):
    return jnp.dot(a, b, preferred_element_type=F32)


def dot_nt(a, b):
    return lax.dot_general(a, b, (((1,), (1,)), ((), ())), preferred_element_type=F32)


def dot_tn(a, b):
    return lax.dot_general(a, b, (((0,), (0,)), ((), ())), preferred_element_type=F32)


def iota(shape, dim):
    return lax.broadcasted_iota(jnp.int32, shape, dim)


def to_bf(mask):
    return jnp.where(mask, 1.0, 0.0).astype(BF16)


def position(z):
    return lax.axis_index("leaf") * z.sample + lax.axis_index("sample")


def peer_id(z, p):
    return {"leaf": p // z.sample, "sample": p % z.sample}


def greet_all(z):
    me = position(z)
    barrier = pltpu.get_barrier_semaphore()

    def body(d, carry):
        pl.semaphore_signal(
            barrier, inc=1, device_id=peer_id(z, (me + d) % z.peers), device_id_type=MESH
        )
        return carry

    lax.fori_loop(1, z.peers, body, 0)
    pl.semaphore_wait(barrier, z.peers - 1)


def view(z, ref, p, count):
    if count is None:
        return ref.at[p]
    return ref.at[pl.ds(pl.multiple_of(p * count, count), count)]


def swap_copy(z, src, dst, sems, d, there, here, to, count):
    return pltpu.make_async_remote_copy(
        src_ref=view(z, src, there, count),
        dst_ref=view(z, dst, here, count),
        send_sem=sems[0].at[d],
        recv_sem=sems[1].at[here],
        device_id=peer_id(z, to),
        device_id_type=MESH,
    )


def swap_start(z, src, dst, sems, count):
    me = position(z)

    def body(d, carry):
        p = (me + d) % z.peers
        swap_copy(z, src, dst, sems, d, p, me, p, count).start()
        return carry

    near = z.sample
    lax.fori_loop(near, z.peers, body, 0)
    lax.fori_loop(1, near, body, 0)


def swap_recv(z, src, dst, sems, count):
    me = position(z)

    def body(d, carry):
        q = (me + d) % z.peers
        swap_copy(z, src, dst, sems, d, q, q, q, count).wait_recv()
        return carry

    lax.fori_loop(1, z.peers, body, 0)


def swap_sent(z, src, dst, sems, count):
    me = position(z)

    def body(d, carry):
        q = (me + d) % z.peers
        swap_copy(z, src, dst, sems, d, q, q, q, count).wait_send()
        return carry

    lax.fori_loop(1, z.peers, body, 0)


def keep_own(z, src, dst, count):
    me = position(z)
    where = pl.ds(pl.multiple_of(me * count, count), count)
    dst[where, :] = src[where, :]


def split_pos(z, pos):
    bits = z.rows.bit_length() - 1
    return lax.shift_right_logical(pos, bits), jnp.bitwise_and(pos, z.rows - 1)


def prepare(z, drow, tsend, place):
    me = position(z)
    owner, target = split_pos(z, drow[...])
    mine = iota((z.peers, z.rows), 0) == owner
    before = to_bf(iota((z.rows, z.rows), 0) < iota((z.rows, z.rows), 1))
    counts = dot(to_bf(mine), before)
    rank = jnp.sum(jnp.where(mine, counts, 0.0), axis=0, keepdims=True).astype(jnp.int32)
    place[...] = to_bf(iota((z.slots, z.rows), 0) == owner * z.cap + rank)
    shift = (me % (LANES // z.cap)) * z.cap
    at_lane = to_bf(iota((LANES, z.rows), 0) == rank + shift)
    code = target + 1
    high = lax.shift_right_logical(code, 4).astype(F32)
    low = jnp.bitwise_and(code, 15).astype(F32)
    targets = 16.0 * dot_nt(jnp.where(mine, high, 0.0).astype(BF16), at_lane) + dot_nt(
        jnp.where(mine, low, 0.0).astype(BF16), at_lane
    )
    for p in range(z.peers):
        tsend[p] = targets[p : p + 1, :]


def group_targets(z, trecv, g):
    per = LANES // z.cap
    row = trecv[g * per]
    for j in range(1, per):
        row = row + trecv[g * per + j]
    return row


def dispatch_kernel(z, drow, pts, cot, rot, rcot, trecv, place, tsend, psend, csend, precv, crecv, *sems):
    tsems, psems, csems = sems[0:2], sems[2:4], sems[4:6]
    me = position(z)
    greet_all(z)
    prepare(z, drow, tsend, place)
    trecv[me] = tsend[me]
    swap_start(z, tsend, trecv, tsems, None)
    psend[...] = dot(place[...], pts[...]).astype(BF16)
    swap_start(z, psend, precv, psems, z.cap)
    csend[...] = dot(place[...], cot[...]).astype(BF16)
    swap_start(z, csend, crecv, csems, z.cap)
    keep_own(z, psend, precv, z.cap)
    keep_own(z, csend, crecv, z.cap)
    swap_recv(z, tsend, trecv, tsems, None)
    swap_recv(z, psend, precv, psems, z.cap)

    def gather(recv):
        total = None
        for g in range(z.groups):
            pick = to_bf(
                (iota((z.rows, LANES), 0) + 1).astype(F32) == group_targets(z, trecv, g)
            )
            part = dot(pick, recv[g * LANES : (g + 1) * LANES, :])
            total = part if total is None else total + part
        return total.astype(BF16)

    rot[...] = gather(precv)
    swap_recv(z, csend, crecv, csems, z.cap)
    rcot[...] = gather(crecv)
    swap_sent(z, tsend, trecv, tsems, None)
    swap_sent(z, psend, precv, psems, z.cap)
    swap_sent(z, csend, crecv, csems, z.cap)


def scale_of(matrix):
    return lax.rsqrt(jnp.mean(matrix * matrix, axis=1, keepdims=True) + EPSILON)


def head_mask(feat, h, dim):
    shape = (1, feat) if dim == 1 else (feat, 1)
    return lax.shift_right_logical(iota(shape, dim), 5) == h


def attention_forward(z, qkv, probs, att):
    feat = z.feat
    balls = z.rows // BALL
    root = HEAD_DIM**-0.5

    def body(h, totals):
        mask = head_mask(feat, h, 1)
        out = []
        for b in range(balls):
            rows = slice(b * BALL, (b + 1) * BALL)
            zero = jnp.zeros((), BF16)
            q = jnp.where(mask, qkv[rows, 0:feat], zero)
            v = jnp.where(mask, qkv[rows, 2 * feat : 3 * feat], zero)
            scores = dot_nt(q, qkv[rows, feat : 2 * feat]) * root
            e = jnp.exp(scores - jnp.max(scores, axis=1, keepdims=True))
            p = e * (1.0 / jnp.sum(e, axis=1, keepdims=True))
            probs[h * balls + b] = p
            out.append(totals[b] + dot(p.astype(BF16), v))
        return tuple(out)

    start = tuple(jnp.zeros((BALL, feat), F32) for _ in range(balls))
    totals = lax.fori_loop(0, HEADS, body, start)
    for b in range(balls):
        att[b * BALL : (b + 1) * BALL, :] = totals[b].astype(BF16)


def mlp(z, rc, normed_two, w_up, w_down, up, down):
    rows, feat = z.rows, z.feat
    total = None
    n2t = normed_two.T
    width = z.hid // z.sample
    per_leaf = z.hid // z.leaf
    for c in range(z.sample):
        cols = slice(c * width, (c + 1) * width)
        x = dot(normed_two, w_up[:, cols])
        x2 = x * x
        t = jnp.tanh(GELU_COEF * (x + 0.044715 * x2 * x))
        half = 0.5 * (1.0 + t)
        hidden = (x * half).astype(BF16)
        slope = half + 0.5 * x * (1.0 - t * t) * GELU_COEF * (1.0 + 3.0 * 0.044715 * x2)
        gpre = (dot_nt(rc, w_down[cols, :]) * slope).astype(BF16)
        up[c] = dot(n2t, gpre).astype(up.dtype)
        gdown = dot_tn(hidden, rc).astype(down.dtype)
        for r in range(0, width, z.down):
            row = c * width + r
            leaf, inner = row // per_leaf, row % per_leaf
            s = inner // z.down
            down[s, leaf * z.down : (leaf + 1) * z.down, :] = gdown[r : r + z.down, :]
        part = dot_nt(gpre, w_up[:, cols])
        total = part if total is None else total + part
    return total


def attention_backward(z, qkv, probs, gatt, gqt, gkt, gvt, lo, hi, totals):
    feat = z.feat
    balls = z.rows // BALL
    qt, gt, dkt, dvt = gqt

    def body(h, totals):
        mask = head_mask(feat, h, 1)
        head_rows = pl.ds(pl.multiple_of(h * HEAD_DIM, HEAD_DIM), HEAD_DIM)
        out = []
        for b in range(balls):
            rows = slice(b * BALL, (b + 1) * BALL)
            zero = jnp.zeros((), BF16)
            g = jnp.where(mask, gatt[rows, :], zero)
            k = jnp.where(mask, qkv[rows, feat : 2 * feat], zero)
            p = probs[h * balls + b]
            gp = dot_nt(g, qkv[rows, 2 * feat : 3 * feat])
            delta = jnp.sum(gp * p, axis=1, keepdims=True)
            gs = (p * (gp - delta)).astype(BF16)
            out.append(totals[b] + dot(gs, k))
            dkt[b, head_rows, :] = dot(qt[b, head_rows, :], gs)
            dvt[b, head_rows, :] = dot(gt[b, head_rows, :], p.astype(BF16))
        return tuple(out)

    return lax.fori_loop(lo, hi, body, totals)


def layer_kernel(
    z, rot, rcot, w_qkv, w_out, w_up, w_down, gain_attn, gain_mlp,
    grot, up, down, qo, gains,
    qkv, probs, att, gatt, gqkv, qt, gt, dkt, dvt,
):
    feat = z.feat
    balls = z.rows // BALL
    root = HEAD_DIM**-0.5
    rotated = rot[...].astype(F32)
    scale_one = scale_of(rotated)
    norm_one = rotated * scale_one
    normed_one = (norm_one * gain_attn[...]).astype(BF16)
    qkv[...] = dot(normed_one, w_qkv[...]).astype(BF16)
    attention_forward(z, qkv, probs, att)
    middle = rotated + dot(att[...], w_out[...])
    scale_two = scale_of(middle)
    norm_two = middle * scale_two
    normed_two = (norm_two * gain_mlp[...]).astype(BF16)
    rc = rcot[...]
    gn2 = mlp(z, rc, normed_two, w_up, w_down, up, down)
    gains[1:2, :] = jnp.sum(gn2 * norm_two, axis=0, keepdims=True)
    inner_two = gn2 * gain_mlp[...]
    gmid = rc.astype(F32) + scale_two * (
        inner_two - norm_two * jnp.mean(inner_two * norm_two, axis=1, keepdims=True)
    )
    gmid_low = gmid.astype(BF16)
    qo[3] = dot_tn(att[...], gmid_low).astype(qo.dtype)
    gatt[...] = dot_nt(gmid_low, w_out[...]).astype(BF16)
    for b in range(balls):
        rows = slice(b * BALL, (b + 1) * BALL)
        qt[b] = qkv[rows, 0:feat].T
        gt[b] = gatt[rows, :].T
    totals = tuple(jnp.zeros((BALL, feat), F32) for _ in range(balls))
    totals = attention_backward(z, qkv, probs, gatt, (qt, gt, dkt, dvt), None, None, 0, HEADS, totals)
    for b in range(balls):
        rows = slice(b * BALL, (b + 1) * BALL)
        gqkv[rows, 0:feat] = (totals[b] * root).astype(BF16)
        gqkv[rows, feat : 2 * feat] = (dkt[b] * root).astype(BF16).T
        gqkv[rows, 2 * feat : 3 * feat] = dvt[b].astype(BF16).T
    gn1 = dot_nt(gqkv[...], w_qkv[...])
    gains[0:1, :] = jnp.sum(gn1 * norm_one, axis=0, keepdims=True)
    inner_one = gn1 * gain_attn[...]
    grot[...] = (
        gmid
        + scale_one * (inner_one - norm_one * jnp.mean(inner_one * norm_one, axis=1, keepdims=True))
    ).astype(BF16)
    n1t = normed_one.T
    for c in range(3):
        qo[c] = dot(n1t, gqkv[:, c * feat : (c + 1) * feat]).astype(qo.dtype)


class Family:
    def __init__(self, z, own, refs, sems):
        self.z, self.own = z, own
        self.first, self.far, self.second, self.out3, self.third, self.out4, self.fourth = refs
        self.sems = sems
        self.s = lax.axis_index("sample")
        self.l = lax.axis_index("leaf")
        self.pair = self.s + 1 - 2 * (self.s % 2)
        self.cross = (self.s + 2) % 4

    def copy(self, src, dst, i, j, device):
        return pltpu.make_async_remote_copy(
            src_ref=src,
            dst_ref=dst,
            send_sem=self.sems[0].at[i],
            recv_sem=self.sems[1].at[j],
            device_id=device,
            device_id_type=MESH,
        )

    def step1(self):
        pair = {"sample": self.pair}
        return [
            self.copy(self.own.at[(self.pair + 2) % 4], self.first.at[1], 1, 1, pair),
            self.copy(self.own.at[self.pair], self.first.at[0], 0, 0, pair),
        ]

    def start1(self):
        for c in self.step1():
            c.start()

    def step2(self):
        return self.copy(self.far, self.second, 2, 2, {"sample": self.cross})

    def start2(self):
        far, near = self.step1()
        far.wait_recv()
        total = self.own[self.cross].astype(F32) + self.first[1].astype(F32)
        self.far[...] = total.astype(self.far.dtype)
        self.step2().start()
        near.wait_recv()

    def step3(self, d):
        z = self.z
        there = (self.l + d) % z.leaf
        rows = pl.ds(pl.multiple_of(there * z.block, z.block), z.block)
        return (
            self.copy(
                self.out3.at[rows], self.third.at[self.l], 3 + d, 3 + self.l, {"leaf": there}
            ),
            self.copy(
                self.out3.at[rows], self.third.at[there], 3 + d, 3 + there, {"leaf": there}
            ),
        )

    def start3(self):
        self.step2().wait_recv()
        total = (
            self.own[self.s].astype(F32) + self.first[0].astype(F32) + self.second[...].astype(F32)
        )
        self.out3[...] = total.astype(self.out3.dtype)

        def body(d, carry):
            self.step3(d)[0].start()
            return carry

        lax.fori_loop(1, self.z.leaf, body, 0)

    def step4(self, d):
        z = self.z
        there = (self.s + d) % z.sample
        base = 3 + z.leaf
        return (
            self.copy(self.out4, self.fourth.at[self.s], base + d, base + self.s, {"sample": there}),
            self.copy(self.out4, self.fourth.at[there], base + d, base + there, {"sample": there}),
        )

    def start4(self):
        z = self.z

        def body(d, carry):
            self.step3(d)[1].wait_recv()
            return carry

        lax.fori_loop(1, z.leaf, body, 0)
        rows = pl.ds(pl.multiple_of(self.l * z.block, z.block), z.block)
        self.third[self.l] = self.out3[rows, :]
        total = self.third[0].astype(F32)
        for j in range(1, z.leaf):
            total = total + self.third[j].astype(F32)
        self.out4[...] = total.astype(self.out4.dtype)
        self.fourth[self.s] = self.out4[...]
        for d in range(1, z.sample):
            self.step4(d)[0].start()

    def finish(self):
        for d in range(1, self.z.sample):
            self.step4(d)[1].wait_recv()

    def sent(self):
        for c in self.step1():
            c.wait_send()
        self.step2().wait_send()

        def body(d, carry):
            self.step3(d)[0].wait_send()
            return carry

        lax.fori_loop(1, self.z.leaf, body, 0)
        for d in range(1, self.z.sample):
            self.step4(d)[0].wait_send()


def family_scratch(z):
    f, w = z.feat, z.wire
    return [
        pltpu.VMEM((2, f, f), w),
        pltpu.VMEM((f, f), w),
        pltpu.VMEM((f, f), w),
        pltpu.VMEM((f, f), w),
        pltpu.VMEM((z.leaf, z.block, f), w),
        pltpu.VMEM((z.block, f), w),
        pltpu.VMEM((z.sample, z.block, f), w),
    ]


def family_sems(z):
    count = 3 + z.leaf + z.sample
    return [pltpu.SemaphoreType.DMA((count,)), pltpu.SemaphoreType.DMA((count,))]


def back_rows(z, trecv, grot, bsend):
    for g in range(z.groups):
        row = group_targets(z, trecv, g)
        col = jnp.broadcast_to(row, (128, LANES)).T[:, 0:1]
        pick = to_bf((iota((LANES, z.rows), 1) + 1).astype(F32) == col)
        bsend[g * LANES : (g + 1) * LANES, :] = dot(pick, grot[...]).astype(BF16)


def restore(z, dcol, brecv):
    owner, _ = split_pos(z, dcol[...])
    mine = iota((z.rows, z.peers), 1) == owner
    before = to_bf(iota((z.rows, z.rows), 1) < iota((z.rows, z.rows), 0))
    counts = dot(before, to_bf(mine))
    rank = jnp.sum(jnp.where(mine, counts, 0.0), axis=1, keepdims=True).astype(jnp.int32)
    pick = to_bf(iota((z.rows, z.slots), 1) == owner * z.cap + rank)
    return dot(pick, brecv[...])


class GainSum:
    def __init__(self, z, own, refs, sems):
        self.z, self.own = z, own
        self.a, self.b, self.c, self.ta, self.tb = refs
        self.sems = sems
        s = lax.axis_index("sample")
        self.l = lax.axis_index("leaf")
        self.pair = {"sample": s + 1 - 2 * (s % 2)}
        self.cross = {"sample": (s + 2) % 4}

    def copy(self, src, dst, i, j, device):
        return pltpu.make_async_remote_copy(
            src_ref=src, dst_ref=dst, send_sem=self.sems[0].at[i], recv_sem=self.sems[1].at[j],
            device_id=device, device_id_type=MESH,
        )

    def step1(self):
        return self.copy(self.own, self.a, 0, 0, self.pair)

    def step2(self):
        return self.copy(self.ta, self.b, 1, 1, self.cross)

    def step3(self, d):
        there = (self.l + d) % self.z.leaf
        device = {"leaf": there}
        return (
            self.copy(self.tb, self.c.at[self.l], 2 + d, 2 + self.l, device),
            self.copy(self.tb, self.c.at[there], 2 + d, 2 + there, device),
        )

    def start1(self):
        self.step1().start()

    def start2(self):
        self.step1().wait_recv()
        self.ta[...] = self.own[...] + self.a[...]
        self.step2().start()

    def start3(self):
        self.step2().wait_recv()
        self.tb[...] = self.ta[...] + self.b[...]
        self.c[self.l] = self.tb[...]

        def body(d, carry):
            self.step3(d)[0].start()
            return carry

        lax.fori_loop(1, self.z.leaf, body, 0)

    def finish(self):
        def body(d, carry):
            self.step3(d)[1].wait_recv()
            return carry

        lax.fori_loop(1, self.z.leaf, body, 0)
        total = self.c[0]
        for j in range(1, self.z.leaf):
            total = total + self.c[j]
        return total

    def sent(self):
        self.step1().wait_send()
        self.step2().wait_send()

        def body(d, carry):
            self.step3(d)[0].wait_send()
            return carry

        lax.fori_loop(1, self.z.leaf, body, 0)


def gain_scratch(z):
    f = z.feat
    return [
        pltpu.VMEM((8, f), F32),
        pltpu.VMEM((8, f), F32),
        pltpu.VMEM((z.leaf, 8, f), F32),
        pltpu.VMEM((8, f), F32),
        pltpu.VMEM((8, f), F32),
    ]


def gain_sems(z):
    return [pltpu.SemaphoreType.DMA((2 + z.leaf,)), pltpu.SemaphoreType.DMA((2 + z.leaf,))]


def write_outputs(z, fams, gsum, o_qkv, o_out, o_up, o_down, o_g1, o_g2):
    up, down, qo = fams
    f = z.feat
    inv = z.inv_root
    for s in range(z.sample):
        o_up[:, s * f : (s + 1) * f] = up.fourth[s].astype(F32) * inv
        o_down[s * z.down : (s + 1) * z.down, :] = down.fourth[s].astype(F32) * inv
    for s in range(3):
        o_qkv[:, s * f : (s + 1) * f] = qo.fourth[s].astype(F32) * inv
    o_out[...] = qo.fourth[3].astype(F32) * inv
    me = lax.axis_index("leaf")
    for o, r in ((o_g1, 0), (o_g2, 1)):
        acc = jnp.zeros((1, z.block), F32)
        for j in range(z.leaf):
            acc = jnp.where(me == j, gsum[r : r + 1, j * z.block : (j + 1) * z.block], acc)
        o[...] = acc * inv


def reduce_kernel(z, dcol, trecv, grot, up, down, qo, gains, *refs):
    o_pts, o_qkv, o_out, o_up, o_down, o_g1, o_g2 = refs[:7]
    refs = refs[7:]
    fr = [refs[7 * i : 7 * i + 7] for i in range(3)]
    refs = refs[21:]
    gr, refs = refs[:5], refs[5:]
    bsend, brecv = refs[:2]
    refs = refs[2:]
    fs = [refs[2 * i : 2 * i + 2] for i in range(3)]
    gs, bs = refs[6:8], refs[8:10]
    fams = [Family(z, own, r, s) for own, r, s in zip((up, down, qo), fr, fs)]
    gain = GainSum(z, gains, gr, gs)
    greet_all(z)
    gain.start1()
    for f in fams:
        f.start1()
    back_rows(z, trecv, grot, bsend)
    keep_own(z, bsend, brecv, z.cap)
    swap_start(z, bsend, brecv, bs, z.cap)
    gain.start2()
    for f in fams:
        f.start2()
    gain.start3()
    for f in fams:
        f.start3()
    for f in fams:
        f.start4()
    total = gain.finish()
    swap_recv(z, bsend, brecv, bs, z.cap)
    o_pts[...] = restore(z, dcol, brecv).astype(BF16)
    for f in fams:
        f.finish()
    write_outputs(z, fams, total, o_qkv, o_out, o_up, o_down, o_g1, o_g2)
    gain.sent()
    for f in fams:
        f.sent()
    swap_sent(z, bsend, brecv, bs, z.cap)


def call(kernel, outs, scratch, collective):
    vmem = pl.BlockSpec(memory_space=pltpu.VMEM)

    def run(*args):
        options = dict(vmem_limit_bytes=48 * 1024 * 1024)
        if collective is not None:
            options.update(collective_id=collective, has_side_effects=True)
        return pl.pallas_call(
            kernel,
            out_shape=[jax.ShapeDtypeStruct(s, t) for s, t in outs],
            in_specs=[vmem] * len(args),
            out_specs=[vmem] * len(outs),
            scratch_shapes=scratch,
            compiler_params=pltpu.CompilerParams(**options),
        )(*args)

    return run


def swap_sems(z):
    return [pltpu.SemaphoreType.DMA((z.peers,)), pltpu.SemaphoreType.DMA((z.peers,))]


def layer_scratch(z):
    r, f = z.rows, z.feat
    balls = r // BALL
    return [
        pltpu.VMEM((r, 3 * f), BF16),
        pltpu.VMEM((HEADS * balls, BALL, BALL), F32),
        pltpu.VMEM((r, f), BF16),
        pltpu.VMEM((r, f), BF16),
        pltpu.VMEM((r, 3 * f), BF16),
        pltpu.VMEM((balls, f, BALL), BF16),
        pltpu.VMEM((balls, f, BALL), BF16),
        pltpu.VMEM((balls, f, BALL), F32),
        pltpu.VMEM((balls, f, BALL), F32),
    ]


def local(mesh, points, cotangent, dest_pos, w_qkv, w_out, w_up, w_down, gain_attn, gain_mlp):
    rows, feat = points.shape
    z = Sizes(mesh, rows, feat, w_up.shape[1])
    drow = dest_pos.reshape(1, rows)
    dcol = dest_pos.reshape(rows, 1)
    trow = (z.peers, 1, LANES)
    rot, rcot, trecv = call(
        lambda *r: dispatch_kernel(z, *r),
        [((rows, feat), BF16), ((rows, feat), BF16), (trow, F32)],
        [
            pltpu.VMEM((z.slots, rows), BF16),
            pltpu.VMEM(trow, F32),
            pltpu.VMEM((z.slots, feat), BF16),
            pltpu.VMEM((z.slots, feat), BF16),
            pltpu.VMEM((z.slots, feat), BF16),
            pltpu.VMEM((z.slots, feat), BF16),
        ]
        + swap_sems(z) * 3,
        0,
    )(drow, points, cotangent)
    fam = ((z.sample, feat, feat), z.wire)
    grot, up, down, qo, gains = call(
        lambda *r: layer_kernel(z, *r),
        [((rows, feat), BF16), fam, fam, fam, ((8, feat), F32)],
        layer_scratch(z),
        None,
    )(
        rot, rcot, w_qkv, w_out, w_up, w_down,
        gain_attn.reshape(1, feat), gain_mlp.reshape(1, feat),
    )
    o_pts, o_qkv, o_out, o_up, o_down, o_g1, o_g2 = call(
        lambda *r: reduce_kernel(z, *r),
        [
            ((rows, feat), BF16),
            ((z.block, 3 * feat), F32),
            ((z.block, feat), F32),
            ((z.block, z.hid), F32),
            ((z.hid // z.leaf, feat), F32),
            ((1, z.block), F32),
            ((1, z.block), F32),
        ],
        family_scratch(z) * 3
        + gain_scratch(z)
        + [pltpu.VMEM((z.slots, feat), BF16), pltpu.VMEM((z.slots, feat), BF16)]
        + family_sems(z) * 3
        + gain_sems(z)
        + swap_sems(z),
        1,
    )(dcol, trecv, grot, up, down, qo, gains)
    return (o_pts, o_qkv, o_out, o_up, o_down, o_g1.reshape(z.block), o_g2.reshape(z.block))


def solution(mesh):
    rows = P(("groups", "leaf", "sample"), None)
    leaf = P(("groups", "leaf"), None)
    in_specs = (rows, rows, P(("groups", "leaf", "sample"))) + (P(),) * 6
    out_specs = (rows,) + (leaf,) * 4 + (P(("groups", "leaf")),) * 2
    return jax.shard_map(
        lambda *a: local(mesh, *a),
        mesh=mesh,
        in_specs=in_specs,
        out_specs=out_specs,
        check_vma=False,
    )
```

```python
import math

import jax
import jax.numpy as jnp
from jax import lax
from jax.experimental import pallas as pl
from jax.experimental.pallas import tpu as pltpu
from jax.sharding import PartitionSpec as P

HEADS = 8
BALL = 256
HEAD_DIM = 32
EPSILON = 1e-06
GELU_COEF = math.sqrt(2.0 / math.pi)
LANES = 256
MESH = pl.DeviceIdType.MESH
F32 = jnp.float32
BF16 = jnp.bfloat16


class Sizes:
    def __init__(self, mesh, rows, feat, hid):
        self.leaf = mesh.shape["leaf"]
        self.sample = mesh.shape["sample"]
        self.peers = self.leaf * self.sample
        self.rows = rows
        self.feat = feat
        self.hid = hid
        self.cap = max(16, 2 * rows // self.peers)
        self.slots = self.peers * self.cap
        self.groups = self.slots // LANES
        self.block = feat // self.leaf
        self.wire = BF16 if self.block % 16 == 0 else F32
        self.down = hid // self.peers
        self.inv_root = 1.0 / math.sqrt(rows * self.peers)


def dot(a, b):
    return jnp.dot(a, b, preferred_element_type=F32)


def dot_nt(a, b):
    return lax.dot_general(a, b, (((1,), (1,)), ((), ())), preferred_element_type=F32)


def dot_tn(a, b):
    return lax.dot_general(a, b, (((0,), (0,)), ((), ())), preferred_element_type=F32)


def iota(shape, dim):
    return lax.broadcasted_iota(jnp.int32, shape, dim)


def to_bf(mask):
    return jnp.where(mask, 1.0, 0.0).astype(BF16)


def position(z):
    return lax.axis_index("leaf") * z.sample + lax.axis_index("sample")


def peer_id(z, p):
    return {"leaf": p // z.sample, "sample": p % z.sample}


def greet_all(z):
    me = position(z)
    barrier = pltpu.get_barrier_semaphore()

    def body(d, carry):
        pl.semaphore_signal(
            barrier, inc=1, device_id=peer_id(z, (me + d) % z.peers), device_id_type=MESH
        )
        return carry

    lax.fori_loop(1, z.peers, body, 0)


def greeted(z):
    pl.semaphore_wait(pltpu.get_barrier_semaphore(), z.peers - 1)


def view(z, ref, p, count):
    if count is None:
        return ref.at[p]
    return ref.at[pl.ds(pl.multiple_of(p * count, count), count)]


def swap_copy(z, src, dst, sems, d, there, here, to, count):
    return pltpu.make_async_remote_copy(
        src_ref=view(z, src, there, count),
        dst_ref=view(z, dst, here, count),
        send_sem=sems[0].at[d],
        recv_sem=sems[1].at[here],
        device_id=peer_id(z, to),
        device_id_type=MESH,
    )


def swap_start(z, src, dst, sems, count):
    me = position(z)

    def body(d, carry):
        p = (me + d) % z.peers
        swap_copy(z, src, dst, sems, d, p, me, p, count).start()
        return carry

    near = z.sample
    lax.fori_loop(near, z.peers, body, 0)
    lax.fori_loop(1, near, body, 0)


def swap_recv(z, src, dst, sems, count):
    me = position(z)

    def body(d, carry):
        q = (me + d) % z.peers
        swap_copy(z, src, dst, sems, d, q, q, q, count).wait_recv()
        return carry

    lax.fori_loop(1, z.peers, body, 0)


def swap_sent(z, src, dst, sems, count):
    me = position(z)

    def body(d, carry):
        q = (me + d) % z.peers
        swap_copy(z, src, dst, sems, d, q, q, q, count).wait_send()
        return carry

    lax.fori_loop(1, z.peers, body, 0)


def keep_own(z, src, dst, count):
    me = position(z)
    where = pl.ds(pl.multiple_of(me * count, count), count)
    dst[where, :] = src[where, :]


def split_pos(z, pos):
    bits = z.rows.bit_length() - 1
    return lax.shift_right_logical(pos, bits), jnp.bitwise_and(pos, z.rows - 1)


def prepare(z, pos, tsend, place):
    me = position(z)
    owner, target = split_pos(z, pos)
    mine = iota((z.peers, z.rows), 0) == owner
    before = to_bf(iota((z.rows, z.rows), 0) < iota((z.rows, z.rows), 1))
    counts = dot(to_bf(mine), before)
    rank = jnp.sum(jnp.where(mine, counts, 0.0), axis=0, keepdims=True).astype(jnp.int32)
    place[...] = to_bf(iota((z.slots, z.rows), 0) == owner * z.cap + rank)
    shift = (me % (LANES // z.cap)) * z.cap
    at_lane = to_bf(iota((LANES, z.rows), 0) == rank + shift)
    code = target + 1
    high = lax.shift_right_logical(code, 4).astype(F32)
    low = jnp.bitwise_and(code, 15).astype(F32)
    targets = 16.0 * dot_nt(jnp.where(mine, high, 0.0).astype(BF16), at_lane) + dot_nt(
        jnp.where(mine, low, 0.0).astype(BF16), at_lane
    )
    for p in range(z.peers):
        tsend[p] = targets[p : p + 1, :]


def group_targets(z, trecv, g):
    per = LANES // z.cap
    row = trecv[g * per]
    for j in range(1, per):
        row = row + trecv[g * per + j]
    return row


def group_picks(z, trecv, pick, back):
    for g in range(z.groups):
        row = group_targets(z, trecv, g)
        cols = slice(g * LANES, (g + 1) * LANES)
        pick[:, cols] = to_bf((iota((z.rows, LANES), 0) + 1).astype(F32) == row)
        col = jnp.broadcast_to(row, (128, LANES)).T[:, 0:1]
        back[cols, :] = to_bf((iota((LANES, z.rows), 1) + 1).astype(F32) == col)


def restore_pick(z, pos, restore):
    pos = jnp.broadcast_to(pos.astype(F32), (128, z.rows)).T[:, 0:1].astype(jnp.int32)
    owner, _ = split_pos(z, pos)
    mine = iota((z.rows, z.peers), 1) == owner
    before = to_bf(iota((z.rows, z.rows), 1) < iota((z.rows, z.rows), 0))
    counts = dot(before, to_bf(mine))
    rank = jnp.sum(jnp.where(mine, counts, 0.0), axis=1, keepdims=True).astype(jnp.int32)
    restore[...] = to_bf(iota((z.rows, z.slots), 1) == owner * z.cap + rank)


def scale_of(matrix):
    return lax.rsqrt(jnp.mean(matrix * matrix, axis=1, keepdims=True) + EPSILON)


def head_mask(feat, h, dim):
    shape = (1, feat) if dim == 1 else (feat, 1)
    return lax.shift_right_logical(iota(shape, dim), 5) == h


def attention_forward(z, qkv, probs, att):
    feat = z.feat
    balls = z.rows // BALL
    root = HEAD_DIM**-0.5

    def body(h, totals):
        mask = head_mask(feat, h, 1)
        out = []
        for b in range(balls):
            rows = slice(b * BALL, (b + 1) * BALL)
            zero = jnp.zeros((), BF16)
            q = jnp.where(mask, qkv[rows, 0:feat], zero)
            v = jnp.where(mask, qkv[rows, 2 * feat : 3 * feat], zero)
            scores = dot_nt(q, qkv[rows, feat : 2 * feat]) * root
            e = jnp.exp(scores - jnp.max(scores, axis=1, keepdims=True))
            p = e * (1.0 / jnp.sum(e, axis=1, keepdims=True))
            probs[h * balls + b] = p
            out.append(totals[b] + dot(p.astype(BF16), v))
        return tuple(out)

    start = tuple(jnp.zeros((BALL, feat), F32) for _ in range(balls))
    totals = lax.fori_loop(0, HEADS, body, start)
    for b in range(balls):
        att[b * BALL : (b + 1) * BALL, :] = totals[b].astype(BF16)


def mlp_forward(z, normed_two, w_up, hidden, slope):
    width = z.hid // z.sample
    for c in range(z.sample):
        cols = slice(c * width, (c + 1) * width)
        x = dot(normed_two, w_up[:, cols])
        x2 = x * x
        t = jnp.tanh(GELU_COEF * (x + 0.044715 * x2 * x))
        half = 0.5 * (1.0 + t)
        hidden[:, cols] = (x * half).astype(BF16)
        slope[:, cols] = half + 0.5 * x * (1.0 - t * t) * GELU_COEF * (
            1.0 + 3.0 * 0.044715 * x2
        )


def mlp_backward(z, rc, n2t, hidden, slope, w_up, w_down, up, down):
    total = None
    width = z.hid // z.sample
    per_leaf = z.hid // z.leaf
    for c in range(z.sample):
        cols = slice(c * width, (c + 1) * width)
        gpre = (dot_nt(rc, w_down[cols, :]) * slope[:, cols]).astype(BF16)
        up[c] = dot(n2t, gpre).astype(up.dtype)
        gdown = dot_tn(hidden[:, cols], rc).astype(down.dtype)
        for r in range(0, width, z.down):
            row = c * width + r
            leaf, inner = row // per_leaf, row % per_leaf
            s = inner // z.down
            down[s, leaf * z.down : (leaf + 1) * z.down, :] = gdown[r : r + z.down, :]
        part = dot_nt(gpre, w_up[:, cols])
        total = part if total is None else total + part
    return total


def attention_backward(z, qkv, probs, gatt, turned, lo, hi, totals):
    feat = z.feat
    balls = z.rows // BALL
    qt, gt, dkt, dvt = turned

    def body(h, totals):
        mask = head_mask(feat, h, 1)
        head_rows = pl.ds(pl.multiple_of(h * HEAD_DIM, HEAD_DIM), HEAD_DIM)
        out = []
        for b in range(balls):
            rows = slice(b * BALL, (b + 1) * BALL)
            zero = jnp.zeros((), BF16)
            g = jnp.where(mask, gatt[rows, :], zero)
            k = jnp.where(mask, qkv[rows, feat : 2 * feat], zero)
            p = probs[h * balls + b]
            gp = dot_nt(g, qkv[rows, 2 * feat : 3 * feat])
            delta = jnp.sum(gp * p, axis=1, keepdims=True)
            gs = (p * (gp - delta)).astype(BF16)
            out.append(totals[b] + dot(gs, k))
            dkt[b, head_rows, :] = dot(qt[b, head_rows, :], gs)
            dvt[b, head_rows, :] = dot(gt[b, head_rows, :], p.astype(BF16))
        return tuple(out)

    return lax.fori_loop(lo, hi, body, totals)


class Family:
    def __init__(self, z, own, refs, sems):
        self.z, self.own = z, own
        self.first, self.far, self.second, self.out3, self.third, self.out4, self.fourth = refs
        self.sems = sems
        self.s = lax.axis_index("sample")
        self.l = lax.axis_index("leaf")
        self.pair = self.s + 1 - 2 * (self.s % 2)
        self.cross = (self.s + 2) % 4

    def copy(self, src, dst, i, j, device):
        return pltpu.make_async_remote_copy(
            src_ref=src,
            dst_ref=dst,
            send_sem=self.sems[0].at[i],
            recv_sem=self.sems[1].at[j],
            device_id=device,
            device_id_type=MESH,
        )

    def step1(self):
        pair = {"sample": self.pair}
        return [
            self.copy(self.own.at[(self.pair + 2) % 4], self.first.at[1], 1, 1, pair),
            self.copy(self.own.at[self.pair], self.first.at[0], 0, 0, pair),
        ]

    def start1(self):
        for c in self.step1():
            c.start()

    def step2(self):
        return self.copy(self.far, self.second, 2, 2, {"sample": self.cross})

    def start2(self):
        far, near = self.step1()
        far.wait_recv()
        total = self.own[self.cross].astype(F32) + self.first[1].astype(F32)
        self.far[...] = total.astype(self.far.dtype)
        self.step2().start()
        near.wait_recv()

    def step3(self, d, source=None):
        z = self.z
        there = (self.l + d) % z.leaf
        slot = self.l if source is None else there
        rows = pl.ds(pl.multiple_of(there * z.block, z.block), z.block)
        return self.copy(
            self.out3.at[rows], self.third.at[slot], 3 + d, 3 + slot, {"leaf": there}
        )

    def start3(self):
        self.step2().wait_recv()
        total = (
            self.own[self.s].astype(F32) + self.first[0].astype(F32) + self.second[...].astype(F32)
        )
        self.out3[...] = total.astype(self.out3.dtype)

        def body(d, carry):
            self.step3(d).start()
            return carry

        lax.fori_loop(1, self.z.leaf, body, 0)

    def step4(self, d, source=None):
        z = self.z
        there = (self.s + d) % z.sample
        slot = self.s if source is None else there
        base = 3 + z.leaf
        return self.copy(self.out4, self.fourth.at[slot], base + d, base + slot, {"sample": there})

    def start4(self):
        z = self.z

        def body(d, carry):
            self.step3(d, 1).wait_recv()
            return carry

        lax.fori_loop(1, z.leaf, body, 0)
        rows = pl.ds(pl.multiple_of(self.l * z.block, z.block), z.block)
        self.third[self.l] = self.out3[rows, :]
        total = self.third[0].astype(F32)
        for j in range(1, z.leaf):
            total = total + self.third[j].astype(F32)
        self.out4[...] = total.astype(self.out4.dtype)
        self.fourth[self.s] = self.out4[...]
        for d in range(1, z.sample):
            self.step4(d).start()

    def finish(self):
        for d in range(1, self.z.sample):
            self.step4(d, 1).wait_recv()

    def sent(self):
        for c in self.step1():
            c.wait_send()
        self.step2().wait_send()

        def body(d, carry):
            self.step3(d).wait_send()
            return carry

        lax.fori_loop(1, self.z.leaf, body, 0)
        for d in range(1, self.z.sample):
            self.step4(d).wait_send()


def family_scratch(z):
    f, w = z.feat, z.wire
    return [
        pltpu.VMEM((2, f, f), w),
        pltpu.VMEM((f, f), w),
        pltpu.VMEM((f, f), w),
        pltpu.VMEM((f, f), w),
        pltpu.VMEM((z.leaf, z.block, f), w),
        pltpu.VMEM((z.block, f), w),
    ]


def family_sems(z):
    count = 3 + z.leaf + z.sample
    return [pltpu.SemaphoreType.DMA((count,)), pltpu.SemaphoreType.DMA((count,))]


class GainSum:
    def __init__(self, z, own, refs, sems):
        self.z, self.own = z, own
        self.a, self.b, self.c, self.ta, self.tb = refs
        self.sems = sems
        s = lax.axis_index("sample")
        self.l = lax.axis_index("leaf")
        self.pair = {"sample": s + 1 - 2 * (s % 2)}
        self.cross = {"sample": (s + 2) % 4}

    def copy(self, src, dst, i, j, device):
        return pltpu.make_async_remote_copy(
            src_ref=src, dst_ref=dst, send_sem=self.sems[0].at[i], recv_sem=self.sems[1].at[j],
            device_id=device, device_id_type=MESH,
        )

    def step1(self):
        return self.copy(self.own, self.a, 0, 0, self.pair)

    def step2(self):
        return self.copy(self.ta, self.b, 1, 1, self.cross)

    def step3(self, d, source=None):
        there = (self.l + d) % self.z.leaf
        slot = self.l if source is None else there
        return self.copy(self.tb, self.c.at[slot], 2 + d, 2 + slot, {"leaf": there})

    def start1(self):
        self.step1().start()

    def start2(self):
        self.step1().wait_recv()
        self.ta[...] = self.own[...] + self.a[...]
        self.step2().start()

    def start3(self):
        self.step2().wait_recv()
        self.tb[...] = self.ta[...] + self.b[...]
        self.c[self.l] = self.tb[...]

        def body(d, carry):
            self.step3(d).start()
            return carry

        lax.fori_loop(1, self.z.leaf, body, 0)

    def finish(self):
        def body(d, carry):
            self.step3(d, 1).wait_recv()
            return carry

        lax.fori_loop(1, self.z.leaf, body, 0)
        total = self.c[0]
        for j in range(1, self.z.leaf):
            total = total + self.c[j]
        return total

    def sent(self):
        self.step1().wait_send()
        self.step2().wait_send()

        def body(d, carry):
            self.step3(d).wait_send()
            return carry

        lax.fori_loop(1, self.z.leaf, body, 0)


def gain_scratch(z):
    f = z.feat
    return [
        pltpu.VMEM((8, f), F32),
        pltpu.VMEM((8, f), F32),
        pltpu.VMEM((z.leaf, 8, f), F32),
        pltpu.VMEM((8, f), F32),
        pltpu.VMEM((8, f), F32),
    ]


def gain_sems(z):
    return [pltpu.SemaphoreType.DMA((2 + z.leaf,)), pltpu.SemaphoreType.DMA((2 + z.leaf,))]


class Take:
    def __init__(self, items):
        self.items = list(items)

    def __call__(self, count):
        head, self.items = self.items[:count], self.items[count:]
        return head


def fused_kernel(z, *refs):
    take = Take(refs)
    drow, gain_attn, gain_mlp = take(3)
    outside = take(6)
    o_pts, up_fourth, down_fourth, qo_fourth, gsum = take(5)
    pts, cot, w_qkv, w_out, w_up, w_down = inside = take(6)
    fr = [take(6) + [last] for last in (up_fourth, down_fourth, qo_fourth)]
    gr = take(5)
    up, down, qo, gains = take(4)
    place, pick, back, restore = take(4)
    tsend, trecv, psend, csend, precv, crecv, bsend, brecv = take(8)
    qkv, probs, att, gatt, gqkv, qt, gt, dkt, dvt, hidden, slope = take(11)
    fs = [take(2) for _ in range(3)]
    gs, ts, ps, cs, bs = take(2), take(2), take(2), take(2), take(2)
    (ls,) = take(1)
    loads = [pltpu.make_async_copy(a, b, ls.at[i]) for i, (a, b) in enumerate(zip(outside, inside))]

    me = position(z)
    feat = z.feat
    balls = z.rows // BALL
    root = HEAD_DIM**-0.5
    fams = [Family(z, own, r, s) for own, r, s in zip((up, down, qo), fr, fs)]
    fup, fdown, fqo = fams
    gain = GainSum(z, gains, gr, gs)

    greet_all(z)
    for load in loads:
        load.start()
    pos = drow[...]
    prepare(z, pos, tsend, place)
    trecv[me] = tsend[me]
    loads[0].wait()
    psend[...] = dot(place[...], pts[...]).astype(BF16)
    greeted(z)
    swap_start(z, tsend, trecv, ts, None)
    swap_start(z, psend, precv, ps, z.cap)
    loads[1].wait()
    csend[...] = dot(place[...], cot[...]).astype(BF16)
    swap_start(z, csend, crecv, cs, z.cap)
    keep_own(z, psend, precv, z.cap)
    keep_own(z, csend, crecv, z.cap)
    restore_pick(z, pos, restore)
    swap_recv(z, tsend, trecv, ts, None)
    group_picks(z, trecv, pick, back)
    for load in loads[2:]:
        load.wait()
    swap_recv(z, psend, precv, ps, z.cap)

    rotated = dot(pick[...], precv[...])
    scale_one = scale_of(rotated)
    norm_one = rotated * scale_one
    normed_one = (norm_one * gain_attn[...]).astype(BF16)
    qkv[...] = dot(normed_one, w_qkv[...]).astype(BF16)
    attention_forward(z, qkv, probs, att)
    middle = rotated + dot(att[...], w_out[...])
    scale_two = scale_of(middle)
    norm_two = middle * scale_two
    normed_two = (norm_two * gain_mlp[...]).astype(BF16)
    mlp_forward(z, normed_two, w_up, hidden, slope)
    n2t = normed_two.T
    n1t = normed_one.T
    for b in range(balls):
        qt[b] = qkv[b * BALL : (b + 1) * BALL, 0:feat].T

    swap_recv(z, csend, crecv, cs, z.cap)
    rcf = dot(pick[...], crecv[...])
    gn2 = mlp_backward(z, rcf.astype(BF16), n2t, hidden, slope, w_up, w_down, up, down)
    fup.start1()
    fdown.start1()
    gains[...] = jnp.zeros((8, feat), F32)
    gains[1:2, :] = jnp.sum(gn2 * norm_two, axis=0, keepdims=True)
    inner_two = gn2 * gain_mlp[...]
    gmid = rcf + scale_two * (
        inner_two - norm_two * jnp.mean(inner_two * norm_two, axis=1, keepdims=True)
    )
    gmid_low = gmid.astype(BF16)
    qo[3] = dot_tn(att[...], gmid_low).astype(qo.dtype)
    gatt[...] = dot_nt(gmid_low, w_out[...]).astype(BF16)
    for b in range(balls):
        gt[b] = gatt[b * BALL : (b + 1) * BALL, :].T
    totals = tuple(jnp.zeros((BALL, feat), F32) for _ in range(balls))
    turned = (qt, gt, dkt, dvt)
    totals = attention_backward(z, qkv, probs, gatt, turned, 0, HEADS // 2, totals)
    fup.start2()
    fdown.start2()
    totals = attention_backward(z, qkv, probs, gatt, turned, HEADS // 2, HEADS, totals)
    fup.start3()
    fdown.start3()
    for b in range(balls):
        rows = slice(b * BALL, (b + 1) * BALL)
        gqkv[rows, 0:feat] = (totals[b] * root).astype(BF16)
        gqkv[rows, feat : 2 * feat] = (dkt[b] * root).astype(BF16).T
        gqkv[rows, 2 * feat : 3 * feat] = dvt[b].astype(BF16).T
    gn1 = dot_nt(gqkv[...], w_qkv[...])
    gains[0:1, :] = jnp.sum(gn1 * norm_one, axis=0, keepdims=True)
    inner_one = gn1 * gain_attn[...]
    grot = (
        gmid
        + scale_one * (inner_one - norm_one * jnp.mean(inner_one * norm_one, axis=1, keepdims=True))
    ).astype(BF16)
    bsend[...] = dot(back[...], grot).astype(BF16)
    swap_start(z, bsend, brecv, bs, z.cap)
    for c in range(3):
        qo[c] = dot(n1t, gqkv[:, c * feat : (c + 1) * feat]).astype(qo.dtype)
    fqo.start1()
    gain.start1()
    keep_own(z, bsend, brecv, z.cap)
    fup.start4()
    fdown.start4()
    fqo.start2()
    gain.start2()
    fqo.start3()
    gain.start3()
    fqo.start4()
    gsum[...] = gain.finish()
    swap_recv(z, bsend, brecv, bs, z.cap)
    o_pts[...] = dot(restore[...], brecv[...]).astype(BF16)
    for f in fams:
        f.finish()
    for f in fams:
        f.sent()
    gain.sent()
    swap_sent(z, tsend, trecv, ts, None)
    swap_sent(z, psend, precv, ps, z.cap)
    swap_sent(z, csend, crecv, cs, z.cap)
    swap_sent(z, bsend, brecv, bs, z.cap)


def finish_kernel(z, pts, up, down, qo, gsum, o_pts, o_qkv, o_out, o_up, o_down, o_g1, o_g2):
    f = z.feat
    inv = z.inv_root
    o_pts[...] = pts[...]
    for s in range(z.sample):
        o_up[:, s * f : (s + 1) * f] = up[s].astype(F32) * inv
        o_down[s * z.down : (s + 1) * z.down, :] = down[s].astype(F32) * inv
    for s in range(3):
        o_qkv[:, s * f : (s + 1) * f] = qo[s].astype(F32) * inv
    o_out[...] = qo[3].astype(F32) * inv
    me = lax.axis_index("leaf")
    for o, r in ((o_g1, 0), (o_g2, 1)):
        acc = jnp.zeros((1, z.block), F32)
        for j in range(z.leaf):
            acc = jnp.where(me == j, gsum[r : r + 1, j * z.block : (j + 1) * z.block], acc)
        o[...] = acc * inv


def call(kernel, outs, scratch, collective, near=None):
    vmem = pl.BlockSpec(memory_space=pltpu.VMEM)
    far = pl.BlockSpec(memory_space=pl.ANY)

    def run(*args):
        count = len(args) if near is None else near
        options = {}
        if collective is not None:
            options = dict(
                vmem_limit_bytes=48 * 1024 * 1024, collective_id=collective, has_side_effects=True
            )
        return pl.pallas_call(
            kernel,
            out_shape=[jax.ShapeDtypeStruct(s, t) for s, t in outs],
            in_specs=[vmem] * count + [far] * (len(args) - count),
            out_specs=[vmem] * len(outs),
            scratch_shapes=scratch,
            compiler_params=pltpu.CompilerParams(**options),
        )(*args)

    return run


def swap_sems(z):
    return [pltpu.SemaphoreType.DMA((z.peers,)), pltpu.SemaphoreType.DMA((z.peers,))]


def layer_scratch(z):
    r, f = z.rows, z.feat
    balls = r // BALL
    return [
        pltpu.VMEM((r, 3 * f), BF16),
        pltpu.VMEM((HEADS * balls, BALL, BALL), F32),
        pltpu.VMEM((r, f), BF16),
        pltpu.VMEM((r, f), BF16),
        pltpu.VMEM((r, 3 * f), BF16),
        pltpu.VMEM((balls, f, BALL), BF16),
        pltpu.VMEM((balls, f, BALL), BF16),
        pltpu.VMEM((balls, f, BALL), F32),
        pltpu.VMEM((balls, f, BALL), F32),
        pltpu.VMEM((r, z.hid), BF16),
        pltpu.VMEM((r, z.hid), F32),
    ]


def local(mesh, points, cotangent, dest_pos, w_qkv, w_out, w_up, w_down, gain_attn, gain_mlp):
    rows, feat = points.shape
    z = Sizes(mesh, rows, feat, w_up.shape[1])
    trow = (z.peers, 1, LANES)
    fam = (z.sample, feat, feat)
    last = ((z.sample, z.block, feat), z.wire)
    outside = (points, cotangent, w_qkv, w_out, w_up, w_down)
    slots = pltpu.VMEM((z.slots, feat), BF16)
    scratch = (
        [pltpu.VMEM(a.shape, a.dtype) for a in outside]
        + family_scratch(z) * 3
        + gain_scratch(z)
        + [pltpu.VMEM(fam, z.wire)] * 3
        + [pltpu.VMEM((8, feat), F32)]
        + [pltpu.VMEM(s, BF16) for s in ((z.slots, rows), (rows, z.slots)) * 2]
        + [pltpu.VMEM(trow, F32)] * 2
        + [slots] * 6
        + layer_scratch(z)
        + family_sems(z) * 3
        + gain_sems(z)
        + swap_sems(z) * 4
        + [pltpu.SemaphoreType.DMA((len(outside),))]
    )
    parts = call(
        lambda *r: fused_kernel(z, *r),
        [((rows, feat), BF16), last, last, last, ((8, feat), F32)],
        scratch,
        0,
        3,
    )(
        dest_pos.reshape(1, rows), gain_attn.reshape(1, feat), gain_mlp.reshape(1, feat), *outside
    )
    o_pts, o_qkv, o_out, o_up, o_down, o_g1, o_g2 = call(
        lambda *r: finish_kernel(z, *r),
        [
            ((rows, feat), BF16),
            ((z.block, 3 * feat), F32),
            ((z.block, feat), F32),
            ((z.block, z.hid), F32),
            ((z.hid // z.leaf, feat), F32),
            ((1, z.block), F32),
            ((1, z.block), F32),
        ],
        [],
        None,
    )(*parts)
    return (o_pts, o_qkv, o_out, o_up, o_down, o_g1.reshape(z.block), o_g2.reshape(z.block))


def solution(mesh):
    rows = P(("groups", "leaf", "sample"), None)
    leaf = P(("groups", "leaf"), None)
    in_specs = (rows, rows, P(("groups", "leaf", "sample"))) + (P(),) * 6
    out_specs = (rows,) + (leaf,) * 4 + (P(("groups", "leaf")),) * 2
    return jax.shard_map(
        lambda *a: local(mesh, *a),
        mesh=mesh,
        in_specs=in_specs,
        out_specs=out_specs,
        check_vma=False,
    )
```

```python
import math

import jax
import jax.numpy as jnp
from jax import lax
from jax.experimental import pallas as pl
from jax.experimental.pallas import tpu as pltpu
from jax.sharding import PartitionSpec as P

HEADS = 8
BALL = 256
HEAD_DIM = 32
EPSILON = 1e-06
GELU_COEF = math.sqrt(2.0 / math.pi)
LANES = 256
UNROLL = 4
VMEM_BYTES = 63 * 1024 * 1024
MESH = pl.DeviceIdType.MESH
F32 = jnp.float32
BF16 = jnp.bfloat16


class Sizes:
    def __init__(self, mesh, rows, feat, hid):
        self.leaf = mesh.shape["leaf"]
        self.sample = mesh.shape["sample"]
        self.peers = self.leaf * self.sample
        self.rows = rows
        self.feat = feat
        self.hid = hid
        self.cap = max(16, 2 * rows // self.peers)
        self.slots = self.peers * self.cap
        self.groups = self.slots // LANES
        self.block = feat // self.leaf
        self.wire = BF16 if self.block % 16 == 0 else F32
        self.down = hid // self.peers
        self.inv_root = 1.0 / math.sqrt(rows * self.peers)


def dot(a, b):
    return jnp.dot(a, b, preferred_element_type=F32)


def dot_nt(a, b):
    return lax.dot_general(a, b, (((1,), (1,)), ((), ())), preferred_element_type=F32)


def dot_tn(a, b):
    return lax.dot_general(a, b, (((0,), (0,)), ((), ())), preferred_element_type=F32)


def iota(shape, dim):
    return lax.broadcasted_iota(jnp.int32, shape, dim)


def to_bf(mask):
    return jnp.where(mask, 1.0, 0.0).astype(BF16)


def position(z):
    return lax.axis_index("leaf") * z.sample + lax.axis_index("sample")


def peer_id(z, p):
    return {"leaf": p // z.sample, "sample": p % z.sample}


def greet_all(z):
    me = position(z)
    barrier = pltpu.get_barrier_semaphore()

    def body(d, carry):
        pl.semaphore_signal(
            barrier, inc=1, device_id=peer_id(z, (me + d) % z.peers), device_id_type=MESH
        )
        return carry

    lax.fori_loop(1, z.peers, body, 0)


def greeted(z):
    pl.semaphore_wait(pltpu.get_barrier_semaphore(), z.peers - 1)


def view(z, ref, p, count):
    if count is None:
        return ref.at[p]
    return ref.at[pl.ds(pl.multiple_of(p * count, count), count)]


def swap_copy(z, src, dst, sems, d, there, here, to, count):
    return pltpu.make_async_remote_copy(
        src_ref=view(z, src, there, count),
        dst_ref=view(z, dst, here, count),
        send_sem=sems[0].at[d],
        recv_sem=sems[1].at[here],
        device_id=peer_id(z, to),
        device_id_type=MESH,
    )


def swap_start(z, src, dst, sems, count):
    me = position(z)

    def body(d, carry):
        p = (me + d) % z.peers
        swap_copy(z, src, dst, sems, d, p, me, p, count).start()
        return carry

    near = z.sample
    lax.fori_loop(near, z.peers, body, 0)
    lax.fori_loop(1, near, body, 0)


def swap_recv(z, src, dst, sems, count):
    me = position(z)

    def body(d, carry):
        q = (me + d) % z.peers
        swap_copy(z, src, dst, sems, d, q, q, q, count).wait_recv()
        return carry

    lax.fori_loop(1, z.peers, body, 0)


def swap_sent(z, src, dst, sems, count):
    me = position(z)

    def body(d, carry):
        q = (me + d) % z.peers
        swap_copy(z, src, dst, sems, d, q, q, q, count).wait_send()
        return carry

    lax.fori_loop(1, z.peers, body, 0)


def keep_own(z, src, dst, count):
    me = position(z)
    where = pl.ds(pl.multiple_of(me * count, count), count)
    dst[where, :] = src[where, :]


def split_pos(z, pos):
    bits = z.rows.bit_length() - 1
    return lax.shift_right_logical(pos, bits), jnp.bitwise_and(pos, z.rows - 1)


def prepare(z, pos, tsend, place):
    me = position(z)
    owner, target = split_pos(z, pos)
    mine = iota((z.peers, z.rows), 0) == owner
    before = to_bf(iota((z.rows, z.rows), 0) < iota((z.rows, z.rows), 1))
    counts = dot(to_bf(mine), before)
    rank = jnp.sum(jnp.where(mine, counts, 0.0), axis=0, keepdims=True).astype(jnp.int32)
    place[...] = to_bf(iota((z.slots, z.rows), 0) == owner * z.cap + rank)
    shift = (me % (LANES // z.cap)) * z.cap
    at_lane = to_bf(iota((LANES, z.rows), 0) == rank + shift)
    code = target + 1
    high = lax.shift_right_logical(code, 4).astype(F32)
    low = jnp.bitwise_and(code, 15).astype(F32)
    targets = 16.0 * dot_nt(jnp.where(mine, high, 0.0).astype(BF16), at_lane) + dot_nt(
        jnp.where(mine, low, 0.0).astype(BF16), at_lane
    )
    for p in range(z.peers):
        tsend[p] = targets[p : p + 1, :]


def group_targets(z, trecv, g):
    per = LANES // z.cap
    row = trecv[g * per]
    for j in range(1, per):
        row = row + trecv[g * per + j]
    return row


def group_picks(z, trecv, pick, back):
    for g in range(z.groups):
        row = group_targets(z, trecv, g)
        cols = slice(g * LANES, (g + 1) * LANES)
        pick[:, cols] = to_bf((iota((z.rows, LANES), 0) + 1).astype(F32) == row)
        col = jnp.broadcast_to(row, (128, LANES)).T[:, 0:1]
        back[cols, :] = to_bf((iota((LANES, z.rows), 1) + 1).astype(F32) == col)


def restore_pick(z, pos, restore):
    pos = jnp.broadcast_to(pos.astype(F32), (128, z.rows)).T[:, 0:1].astype(jnp.int32)
    owner, _ = split_pos(z, pos)
    mine = iota((z.rows, z.peers), 1) == owner
    before = to_bf(iota((z.rows, z.rows), 1) < iota((z.rows, z.rows), 0))
    counts = dot(before, to_bf(mine))
    rank = jnp.sum(jnp.where(mine, counts, 0.0), axis=1, keepdims=True).astype(jnp.int32)
    restore[...] = to_bf(iota((z.rows, z.slots), 1) == owner * z.cap + rank)


def scale_of(matrix):
    return lax.rsqrt(jnp.mean(matrix * matrix, axis=1, keepdims=True) + EPSILON)


def head_mask(feat, h, dim):
    shape = (1, feat) if dim == 1 else (feat, 1)
    return lax.shift_right_logical(iota(shape, dim), 5) == h


def attention_forward(z, qkv, probs, att):
    feat = z.feat
    balls = z.rows // BALL
    root = HEAD_DIM**-0.5

    def body(h, totals):
        mask = head_mask(feat, h, 1)
        out = []
        for b in range(balls):
            rows = slice(b * BALL, (b + 1) * BALL)
            zero = jnp.zeros((), BF16)
            q = jnp.where(mask, qkv[rows, 0:feat], zero)
            v = jnp.where(mask, qkv[rows, 2 * feat : 3 * feat], zero)
            scores = dot_nt(q, qkv[rows, feat : 2 * feat]) * root
            e = jnp.exp(scores - jnp.max(scores, axis=1, keepdims=True))
            p = e * (1.0 / jnp.sum(e, axis=1, keepdims=True))
            probs[h * balls + b] = p
            out.append(totals[b] + dot(p.astype(BF16), v))
        return tuple(out)

    start = tuple(jnp.zeros((BALL, feat), F32) for _ in range(balls))
    totals = lax.fori_loop(0, HEADS, body, start, unroll=UNROLL)
    for b in range(balls):
        att[b * BALL : (b + 1) * BALL, :] = totals[b].astype(BF16)


def mlp_forward(z, normed_two, w_up, hidden, slope):
    width = z.hid // z.sample
    for c in range(z.sample):
        cols = slice(c * width, (c + 1) * width)
        x = dot(normed_two, w_up[:, cols])
        x2 = x * x
        t = jnp.tanh(GELU_COEF * (x + 0.044715 * x2 * x))
        half = 0.5 * (1.0 + t)
        hidden[:, cols] = (x * half).astype(BF16)
        slope[:, cols] = half + 0.5 * x * (1.0 - t * t) * GELU_COEF * (
            1.0 + 3.0 * 0.044715 * x2
        )


def mlp_backward(z, rc, n2t, hidden, slope, w_up, w_down, up, down):
    total = None
    width = z.hid // z.sample
    per_leaf = z.hid // z.leaf
    for c in range(z.sample):
        cols = slice(c * width, (c + 1) * width)
        gpre = (dot_nt(rc, w_down[cols, :]) * slope[:, cols]).astype(BF16)
        up[c] = dot(n2t, gpre).astype(up.dtype)
        gdown = dot_tn(hidden[:, cols], rc).astype(down.dtype)
        for r in range(0, width, z.down):
            row = c * width + r
            leaf, inner = row // per_leaf, row % per_leaf
            s = inner // z.down
            down[s, leaf * z.down : (leaf + 1) * z.down, :] = gdown[r : r + z.down, :]
        part = dot_nt(gpre, w_up[:, cols])
        total = part if total is None else total + part
    return total


def attention_backward(z, qkv, probs, gatt, turned, lo, hi, totals):
    feat = z.feat
    balls = z.rows // BALL
    qt, gt, dkt, dvt = turned

    def body(h, totals):
        mask = head_mask(feat, h, 1)
        head_rows = pl.ds(pl.multiple_of(h * HEAD_DIM, HEAD_DIM), HEAD_DIM)
        out = []
        for b in range(balls):
            rows = slice(b * BALL, (b + 1) * BALL)
            zero = jnp.zeros((), BF16)
            g = jnp.where(mask, gatt[rows, :], zero)
            k = jnp.where(mask, qkv[rows, feat : 2 * feat], zero)
            p = probs[h * balls + b]
            gp = dot_nt(g, qkv[rows, 2 * feat : 3 * feat])
            delta = jnp.sum(gp * p, axis=1, keepdims=True)
            gs = (p * (gp - delta)).astype(BF16)
            out.append(totals[b] + dot(gs, k))
            dkt[b, head_rows, :] = dot(qt[b, head_rows, :], gs)
            dvt[b, head_rows, :] = dot(gt[b, head_rows, :], p.astype(BF16))
        return tuple(out)

    return lax.fori_loop(lo, hi, body, totals, unroll=UNROLL)


class Family:
    def __init__(self, z, own, refs, sems):
        self.z, self.own = z, own
        self.first, self.far, self.second, self.out3, self.third, self.out4, self.fourth = refs
        self.sems = sems
        self.s = lax.axis_index("sample")
        self.l = lax.axis_index("leaf")
        self.pair = self.s + 1 - 2 * (self.s % 2)
        self.cross = (self.s + 2) % 4

    def copy(self, src, dst, i, j, device):
        return pltpu.make_async_remote_copy(
            src_ref=src,
            dst_ref=dst,
            send_sem=self.sems[0].at[i],
            recv_sem=self.sems[1].at[j],
            device_id=device,
            device_id_type=MESH,
        )

    def step1(self):
        pair = {"sample": self.pair}
        return [
            self.copy(self.own.at[(self.pair + 2) % 4], self.first.at[1], 1, 1, pair),
            self.copy(self.own.at[self.pair], self.first.at[0], 0, 0, pair),
        ]

    def start1(self):
        for c in self.step1():
            c.start()

    def step2(self):
        return self.copy(self.far, self.second, 2, 2, {"sample": self.cross})

    def start2(self):
        far, near = self.step1()
        far.wait_recv()
        total = self.own[self.cross].astype(F32) + self.first[1].astype(F32)
        self.far[...] = total.astype(self.far.dtype)
        self.step2().start()
        near.wait_recv()

    def step3(self, d, source=None):
        z = self.z
        there = (self.l + d) % z.leaf
        slot = self.l if source is None else there
        rows = pl.ds(pl.multiple_of(there * z.block, z.block), z.block)
        return self.copy(
            self.out3.at[rows], self.third.at[slot], 3 + d, 3 + slot, {"leaf": there}
        )

    def start3(self):
        self.step2().wait_recv()
        total = (
            self.own[self.s].astype(F32) + self.first[0].astype(F32) + self.second[...].astype(F32)
        )
        self.out3[...] = total.astype(self.out3.dtype)

        def body(d, carry):
            self.step3(d).start()
            return carry

        lax.fori_loop(1, self.z.leaf, body, 0)

    def step4(self, d, source=None):
        z = self.z
        there = (self.s + d) % z.sample
        slot = self.s if source is None else there
        base = 3 + z.leaf
        return self.copy(self.out4, self.fourth.at[slot], base + d, base + slot, {"sample": there})

    def start4(self):
        z = self.z

        def body(d, carry):
            self.step3(d, 1).wait_recv()
            return carry

        lax.fori_loop(1, z.leaf, body, 0)
        rows = pl.ds(pl.multiple_of(self.l * z.block, z.block), z.block)
        self.third[self.l] = self.out3[rows, :]
        total = self.third[0].astype(F32)
        for j in range(1, z.leaf):
            total = total + self.third[j].astype(F32)
        self.out4[...] = total.astype(self.out4.dtype)
        self.fourth[self.s] = self.out4[...]
        for d in range(1, z.sample):
            self.step4(d).start()

    def finish(self):
        for d in range(1, self.z.sample):
            self.step4(d, 1).wait_recv()

    def sent(self):
        for c in self.step1():
            c.wait_send()
        self.step2().wait_send()

        def body(d, carry):
            self.step3(d).wait_send()
            return carry

        lax.fori_loop(1, self.z.leaf, body, 0)
        for d in range(1, self.z.sample):
            self.step4(d).wait_send()


def family_scratch(z):
    f, w = z.feat, z.wire
    return [
        pltpu.VMEM((2, f, f), w),
        pltpu.VMEM((f, f), w),
        pltpu.VMEM((f, f), w),
        pltpu.VMEM((f, f), w),
        pltpu.VMEM((z.leaf, z.block, f), w),
        pltpu.VMEM((z.block, f), w),
    ]


def family_sems(z):
    count = 3 + z.leaf + z.sample
    return [pltpu.SemaphoreType.DMA((count,)), pltpu.SemaphoreType.DMA((count,))]


class GainSum:
    def __init__(self, z, own, refs, sems):
        self.z, self.own = z, own
        self.a, self.b, self.c, self.ta, self.tb = refs
        self.sems = sems
        s = lax.axis_index("sample")
        self.l = lax.axis_index("leaf")
        self.pair = {"sample": s + 1 - 2 * (s % 2)}
        self.cross = {"sample": (s + 2) % 4}

    def copy(self, src, dst, i, j, device):
        return pltpu.make_async_remote_copy(
            src_ref=src, dst_ref=dst, send_sem=self.sems[0].at[i], recv_sem=self.sems[1].at[j],
            device_id=device, device_id_type=MESH,
        )

    def step1(self):
        return self.copy(self.own, self.a, 0, 0, self.pair)

    def step2(self):
        return self.copy(self.ta, self.b, 1, 1, self.cross)

    def step3(self, d, source=None):
        there = (self.l + d) % self.z.leaf
        slot = self.l if source is None else there
        return self.copy(self.tb, self.c.at[slot], 2 + d, 2 + slot, {"leaf": there})

    def start1(self):
        self.step1().start()

    def start2(self):
        self.step1().wait_recv()
        self.ta[...] = self.own[...] + self.a[...]
        self.step2().start()

    def start3(self):
        self.step2().wait_recv()
        self.tb[...] = self.ta[...] + self.b[...]
        self.c[self.l] = self.tb[...]

        def body(d, carry):
            self.step3(d).start()
            return carry

        lax.fori_loop(1, self.z.leaf, body, 0)

    def finish(self):
        def body(d, carry):
            self.step3(d, 1).wait_recv()
            return carry

        lax.fori_loop(1, self.z.leaf, body, 0)
        total = self.c[0]
        for j in range(1, self.z.leaf):
            total = total + self.c[j]
        return total

    def sent(self):
        self.step1().wait_send()
        self.step2().wait_send()

        def body(d, carry):
            self.step3(d).wait_send()
            return carry

        lax.fori_loop(1, self.z.leaf, body, 0)


def gain_scratch(z):
    f = z.feat
    return [
        pltpu.VMEM((8, f), F32),
        pltpu.VMEM((8, f), F32),
        pltpu.VMEM((z.leaf, 8, f), F32),
        pltpu.VMEM((8, f), F32),
        pltpu.VMEM((8, f), F32),
    ]


def gain_sems(z):
    return [pltpu.SemaphoreType.DMA((2 + z.leaf,)), pltpu.SemaphoreType.DMA((2 + z.leaf,))]


class Take:
    def __init__(self, items):
        self.items = list(items)

    def __call__(self, count):
        head, self.items = self.items[:count], self.items[count:]
        return head


def fused_kernel(z, *refs):
    take = Take(refs)
    drow, gain_attn, gain_mlp = take(3)
    outside = take(6)
    o_pts, up_fourth, down_fourth, qo_fourth, gsum = take(5)
    pts, cot, w_qkv, w_out, w_up, w_down = inside = take(6)
    fr = [take(6) + [last] for last in (up_fourth, down_fourth, qo_fourth)]
    gr = take(5)
    up, down, qo, gains = take(4)
    place, pick, back, restore = take(4)
    tsend, trecv, psend, csend, precv, crecv, bsend, brecv = take(8)
    qkv, probs, att, gatt, gqkv, qt, gt, dkt, dvt, hidden, slope = take(11)
    fs = [take(2) for _ in range(3)]
    gs, ts, ps, cs, bs = take(2), take(2), take(2), take(2), take(2)
    (ls,) = take(1)
    loads = [pltpu.make_async_copy(a, b, ls.at[i]) for i, (a, b) in enumerate(zip(outside, inside))]

    me = position(z)
    feat = z.feat
    balls = z.rows // BALL
    root = HEAD_DIM**-0.5
    fams = [Family(z, own, r, s) for own, r, s in zip((up, down, qo), fr, fs)]
    fup, fdown, fqo = fams
    gain = GainSum(z, gains, gr, gs)

    greet_all(z)
    for load in loads:
        load.start()
    pos = drow[...]
    prepare(z, pos, tsend, place)
    trecv[me] = tsend[me]
    loads[0].wait()
    psend[...] = dot(place[...], pts[...]).astype(BF16)
    greeted(z)
    swap_start(z, tsend, trecv, ts, None)
    swap_start(z, psend, precv, ps, z.cap)
    loads[1].wait()
    csend[...] = dot(place[...], cot[...]).astype(BF16)
    swap_start(z, csend, crecv, cs, z.cap)
    keep_own(z, psend, precv, z.cap)
    keep_own(z, csend, crecv, z.cap)
    restore_pick(z, pos, restore)
    swap_recv(z, tsend, trecv, ts, None)
    group_picks(z, trecv, pick, back)
    for load in loads[2:]:
        load.wait()
    swap_recv(z, psend, precv, ps, z.cap)

    rotated = dot(pick[...], precv[...])
    scale_one = scale_of(rotated)
    norm_one = rotated * scale_one
    normed_one = (norm_one * gain_attn[...]).astype(BF16)
    qkv[...] = dot(normed_one, w_qkv[...]).astype(BF16)
    attention_forward(z, qkv, probs, att)
    middle = rotated + dot(att[...], w_out[...])
    scale_two = scale_of(middle)
    norm_two = middle * scale_two
    normed_two = (norm_two * gain_mlp[...]).astype(BF16)
    mlp_forward(z, normed_two, w_up, hidden, slope)
    n2t = normed_two.T
    n1t = normed_one.T
    for b in range(balls):
        qt[b] = qkv[b * BALL : (b + 1) * BALL, 0:feat].T

    swap_recv(z, csend, crecv, cs, z.cap)
    rcf = dot(pick[...], crecv[...])
    gn2 = mlp_backward(z, rcf.astype(BF16), n2t, hidden, slope, w_up, w_down, up, down)
    fup.start1()
    fdown.start1()
    gains[...] = jnp.zeros((8, feat), F32)
    gains[1:2, :] = jnp.sum(gn2 * norm_two, axis=0, keepdims=True)
    inner_two = gn2 * gain_mlp[...]
    gmid = rcf + scale_two * (
        inner_two - norm_two * jnp.mean(inner_two * norm_two, axis=1, keepdims=True)
    )
    gmid_low = gmid.astype(BF16)
    qo[3] = dot_tn(att[...], gmid_low).astype(qo.dtype)
    gatt[...] = dot_nt(gmid_low, w_out[...]).astype(BF16)
    for b in range(balls):
        gt[b] = gatt[b * BALL : (b + 1) * BALL, :].T
    totals = tuple(jnp.zeros((BALL, feat), F32) for _ in range(balls))
    turned = (qt, gt, dkt, dvt)
    totals = attention_backward(z, qkv, probs, gatt, turned, 0, HEADS, totals)
    for b in range(balls):
        rows = slice(b * BALL, (b + 1) * BALL)
        gqkv[rows, 0:feat] = (totals[b] * root).astype(BF16)
        gqkv[rows, feat : 2 * feat] = (dkt[b] * root).astype(BF16).T
        gqkv[rows, 2 * feat : 3 * feat] = dvt[b].astype(BF16).T
    gn1 = dot_nt(gqkv[...], w_qkv[...])
    gains[0:1, :] = jnp.sum(gn1 * norm_one, axis=0, keepdims=True)
    inner_one = gn1 * gain_attn[...]
    grot = (
        gmid
        + scale_one * (inner_one - norm_one * jnp.mean(inner_one * norm_one, axis=1, keepdims=True))
    ).astype(BF16)
    bsend[...] = dot(back[...], grot).astype(BF16)
    swap_start(z, bsend, brecv, bs, z.cap)
    fup.start2()
    fdown.start2()
    for c in range(3):
        qo[c] = dot(n1t, gqkv[:, c * feat : (c + 1) * feat]).astype(qo.dtype)
    fqo.start1()
    gain.start1()
    keep_own(z, bsend, brecv, z.cap)
    fqo.start2()
    gain.start2()
    fup.start3()
    fdown.start3()
    fqo.start3()
    gain.start3()
    fup.start4()
    fdown.start4()
    fqo.start4()
    gsum[...] = gain.finish()
    swap_recv(z, bsend, brecv, bs, z.cap)
    o_pts[...] = dot(restore[...], brecv[...]).astype(BF16)
    for f in fams:
        f.finish()
    for f in fams:
        f.sent()
    gain.sent()
    swap_sent(z, tsend, trecv, ts, None)
    swap_sent(z, psend, precv, ps, z.cap)
    swap_sent(z, csend, crecv, cs, z.cap)
    swap_sent(z, bsend, brecv, bs, z.cap)


def finish_kernel(z, *refs):
    outside, refs = refs[:5], refs[5:]
    (o_pts, o_qkv, o_out, o_up, o_down, o_g1, o_g2), refs = refs[:7], refs[7:]
    pts, up, down, qo, gsum = inside = refs[:5]
    loads = [
        pltpu.make_async_copy(a, b, refs[5].at[i]) for i, (a, b) in enumerate(zip(outside, inside))
    ]
    for load in loads:
        load.start()
    for load in loads:
        load.wait()
    f = z.feat
    inv = z.inv_root
    o_pts[...] = pts[...]
    for s in range(z.sample):
        o_up[:, s * f : (s + 1) * f] = up[s].astype(F32) * inv
        o_down[s * z.down : (s + 1) * z.down, :] = down[s].astype(F32) * inv
    for s in range(3):
        o_qkv[:, s * f : (s + 1) * f] = qo[s].astype(F32) * inv
    o_out[...] = qo[3].astype(F32) * inv
    me = lax.axis_index("leaf")
    for o, r in ((o_g1, 0), (o_g2, 1)):
        acc = jnp.zeros((1, z.block), F32)
        for j in range(z.leaf):
            acc = jnp.where(me == j, gsum[r : r + 1, j * z.block : (j + 1) * z.block], acc)
        o[...] = acc * inv


def call(kernel, outs, scratch, collective, near=None):
    vmem = pl.BlockSpec(memory_space=pltpu.VMEM)
    far = pl.BlockSpec(memory_space=pltpu.HBM)

    def run(*args):
        count = len(args) if near is None else near
        options = dict(vmem_limit_bytes=VMEM_BYTES)
        if collective is not None:
            options.update(collective_id=collective, has_side_effects=True)
        return pl.pallas_call(
            kernel,
            out_shape=[jax.ShapeDtypeStruct(s, t) for s, t in outs],
            in_specs=[vmem] * count + [far] * (len(args) - count),
            out_specs=[vmem] * len(outs),
            scratch_shapes=scratch,
            compiler_params=pltpu.CompilerParams(**options),
        )(*args)

    return run


def swap_sems(z):
    return [pltpu.SemaphoreType.DMA((z.peers,)), pltpu.SemaphoreType.DMA((z.peers,))]


def layer_scratch(z):
    r, f = z.rows, z.feat
    balls = r // BALL
    return [
        pltpu.VMEM((r, 3 * f), BF16),
        pltpu.VMEM((HEADS * balls, BALL, BALL), F32),
        pltpu.VMEM((r, f), BF16),
        pltpu.VMEM((r, f), BF16),
        pltpu.VMEM((r, 3 * f), BF16),
        pltpu.VMEM((balls, f, BALL), BF16),
        pltpu.VMEM((balls, f, BALL), BF16),
        pltpu.VMEM((balls, f, BALL), F32),
        pltpu.VMEM((balls, f, BALL), F32),
        pltpu.VMEM((r, z.hid), BF16),
        pltpu.VMEM((r, z.hid), F32),
    ]


def local(mesh, points, cotangent, dest_pos, w_qkv, w_out, w_up, w_down, gain_attn, gain_mlp):
    rows, feat = points.shape
    z = Sizes(mesh, rows, feat, w_up.shape[1])
    trow = (z.peers, 1, LANES)
    fam = (z.sample, feat, feat)
    last = ((z.sample, z.block, feat), z.wire)
    outside = (points, cotangent, w_qkv, w_out, w_up, w_down)
    slots = pltpu.VMEM((z.slots, feat), BF16)
    scratch = (
        [pltpu.VMEM(a.shape, a.dtype) for a in outside]
        + family_scratch(z) * 3
        + gain_scratch(z)
        + [pltpu.VMEM(fam, z.wire)] * 3
        + [pltpu.VMEM((8, feat), F32)]
        + [pltpu.VMEM(s, BF16) for s in ((z.slots, rows), (rows, z.slots)) * 2]
        + [pltpu.VMEM(trow, F32)] * 2
        + [slots] * 6
        + layer_scratch(z)
        + family_sems(z) * 3
        + gain_sems(z)
        + swap_sems(z) * 4
        + [pltpu.SemaphoreType.DMA((len(outside),))]
    )
    parts = call(
        lambda *r: fused_kernel(z, *r),
        [((rows, feat), BF16), last, last, last, ((8, feat), F32)],
        scratch,
        0,
        3,
    )(
        dest_pos.reshape(1, rows), gain_attn.reshape(1, feat), gain_mlp.reshape(1, feat), *outside
    )
    o_pts, o_qkv, o_out, o_up, o_down, o_g1, o_g2 = call(
        lambda *r: finish_kernel(z, *r),
        [
            ((rows, feat), BF16),
            ((z.block, 3 * feat), F32),
            ((z.block, feat), F32),
            ((z.block, z.hid), F32),
            ((z.hid // z.leaf, feat), F32),
            ((1, z.block), F32),
            ((1, z.block), F32),
        ],
        [pltpu.VMEM(a.shape, a.dtype) for a in parts]
        + [pltpu.SemaphoreType.DMA((len(parts),))],
        None,
        0,
    )(*parts)
    return (o_pts, o_qkv, o_out, o_up, o_down, o_g1.reshape(z.block), o_g2.reshape(z.block))


def solution(mesh):
    rows = P(("groups", "leaf", "sample"), None)
    leaf = P(("groups", "leaf"), None)
    in_specs = (rows, rows, P(("groups", "leaf", "sample"))) + (P(),) * 6
    out_specs = (rows,) + (leaf,) * 4 + (P(("groups", "leaf")),) * 2
    return jax.shard_map(
        lambda *a: local(mesh, *a),
        mesh=mesh,
        in_specs=in_specs,
        out_specs=out_specs,
        check_vma=False,
    )
```
